32 devices in a mesh: parts: 2 (over x), tensor: 16 (over z, y, core).
Axes of the slice: x: 2, y: 2, z: 4, core: 2. Of those that a mesh axis runs over, the one named last changes fastest.
Arguments:
- hidden: bfloat16 [1024, 28672], P('parts', 'tensor'), parts along dimension 0, may hold values from -6 to 6
- frozen_weight: bfloat16 [28672, 8192], P('tensor'), may hold values from -0.03125 to 0.03125
- adapter_input_maps: bfloat16 [64, 16, 28672], P(('parts', 'tensor')), parts along dimension 0, may hold values from -0.03125 to 0.03125
- adapter_output_maps: bfloat16 [64, 16, 8192], P(('parts', 'tensor')), parts along dimension 0, may hold values from -1.5 to 1.5
- adapter_per_block: int32 [128], P('parts'), parts along dimension 0, may hold values from 0 to 31, as said below
- rows_per_block: int32 [128], P('parts'), parts along dimension 0, may hold values from 1 to 8, as said below
- cotangent: bfloat16 [1024, 8192], P('parts', 'tensor'), parts along dimension 0, may hold values from -6 to 6
Outputs:
- output: bfloat16 [1024, 8192], P('parts', 'tensor'), parts along dimension 0
- hidden_gradient: bfloat16 [1024, 28672], P('parts', 'tensor'), parts along dimension 0
- input_map_gradient: float32 [64, 16, 28672], P(('parts', 'tensor')), parts along dimension 0
- output_map_gradient: float32 [64, 16, 8192], P(('parts', 'tensor')), parts along dimension 0
The draws below stay inside these ranges and needn't reach their ends.
There are 2 independent parts, one for each index of `parts`. The reference program is written for one: setup_inputs(seed, part) draws one part's arguments, and reference() takes and returns one part's arrays. A program takes and returns all parts, laid end to end along the dimension named above; an argument that names none is the same for every part. Nothing has to cross between parts.
Inputs may be any that keep to these rules, and one draw needn't show every extreme that they name: `adapter_per_block`: adapter a is held by index a // 2 of tensor. The blocks that name adapters of one holder number at most 8, and exactly 8 for some holder. `rows_per_block`: some block is full.
All inputs are finite; a program needn't handle non-finite values.
Results may differ from the reference program's by a relative error of at most 0.0032.
Values may be sent and summed in bfloat16 or wider, within the bound.
A program may use at most 256 MiB of HBM per device.

```python
import jax
import jax.numpy as jnp
from jax import lax

MODEL_DIM = 8192
HIDDEN_UNITS = 28672
ADAPTER_RANK = 16
ADP_DEV = 2
BLK = 8
TOKENS = 512
ADAPTER_COUNT = 32
NBLK = 64
CAP = 8


def draw_adapter_per_block(key, part):
    key = jax.random.fold_in(key, 11)
    first_key, slots_key, order_key, local_key = jax.random.split(key, 4)
    holders = ADAPTER_COUNT // ADP_DEV
    busiest = jax.random.randint(first_key, (), 0, holders)
    others = jax.random.permutation(slots_key, (holders - 1) * CAP)[:NBLK - CAP]
    other_holder = others // CAP
    other_holder = other_holder + (other_holder >= busiest).astype(jnp.int32)
    holder_list = jnp.concatenate([jnp.full((CAP,), busiest, jnp.int32), other_holder.astype(jnp.int32)])
    holder_list = holder_list[jax.random.permutation(order_key, NBLK)]
    local_pick = jax.random.randint(local_key, (NBLK,), 0, ADP_DEV)
    return (holder_list * ADP_DEV + local_pick).astype(jnp.int32)


def draw_rows_per_block(key, part):
    key = jax.random.fold_in(key, 23)
    rows_key, full_key = jax.random.split(key)
    counts = jax.random.randint(rows_key, (NBLK,), 1, BLK + 1)
    full_at = jax.random.randint(full_key, (), 0, NBLK)
    return jnp.where(jnp.arange(NBLK) == full_at, BLK, counts).astype(jnp.int32)


def level_of(rng, shape, cuts, smallest, high):
    level = 1.0
    for position, shards_of in cuts:
        steps = jax.random.uniform(jax.random.fold_in(jax.random.fold_in(rng, 6), position), (shards_of,), jnp.float32, smallest / len(cuts), high / len(cuts))
        level = level * jnp.repeat(jnp.exp(steps), shape[position] // shards_of).reshape((-1,) + (1,) * (len(shape) - 1 - position))
    return level


def centred(rng, dims, width, bound, pieces=(), held_as=jnp.bfloat16):
    result = jax.random.normal(rng, dims, jnp.float32) * width
    if len(pieces) > 0:
        result = level_of(rng, dims, pieces, -0.22, 0.18) * result
    return jnp.clip(result, min=-bound, max=bound).astype(held_as)


def setup_inputs(seed: int = 0, part: int = 0) -> dict:
    arg_keys = jax.random.split(jax.random.key(seed), 8)
    part_splits = jax.random.split(jax.random.fold_in(arg_keys[7], part), 8)
    return {
        "hidden": centred(part_splits[0], (TOKENS, HIDDEN_UNITS), 1.0, 6.0, ((1, 16),)),
        "frozen_weight": centred(arg_keys[1], (HIDDEN_UNITS, MODEL_DIM), HIDDEN_UNITS ** -0.5, 0.03125, ((0, 16),)),
        "adapter_input_maps": centred(part_splits[2], (ADAPTER_COUNT, ADAPTER_RANK, HIDDEN_UNITS), HIDDEN_UNITS ** -0.5, 0.03125, ((0, 16),)),
        "adapter_output_maps": centred(part_splits[3], (ADAPTER_COUNT, ADAPTER_RANK, MODEL_DIM), ADAPTER_RANK ** -0.5, 1.5, ((0, 16),)),
        "adapter_per_block": draw_adapter_per_block(jax.random.fold_in(jax.random.fold_in(arg_keys[7], part), 71), part),
        "rows_per_block": draw_rows_per_block(jax.random.fold_in(jax.random.fold_in(arg_keys[7], part), 71), part),
        "cotangent": centred(part_splits[6], (TOKENS, MODEL_DIM), 1.0, 6.0, ((1, 16),)),
    }


adapter_scale = 0.5


def reference(hidden, frozen_weight, adapter_input_maps, adapter_output_maps, adapter_per_block, rows_per_block, cotangent):
    live_rows = (jnp.arange(BLK)[None, :] < rows_per_block[:, None]).reshape(TOKENS)
    row_adapter = jnp.repeat(adapter_per_block, BLK, total_repeat_length=TOKENS)
    picker = ((row_adapter[:, None] == jnp.arange(ADAPTER_COUNT)[None, :]) & live_rows[:, None]).astype(jnp.float32)
    flattened_input_maps = adapter_input_maps.reshape(ADAPTER_COUNT * ADAPTER_RANK, HIDDEN_UNITS)
    flattened_output_maps = adapter_output_maps.reshape(ADAPTER_COUNT * ADAPTER_RANK, MODEL_DIM)
    wide_low = jnp.dot(hidden, flattened_input_maps.T, preferred_element_type=jnp.float32)
    low_rank = jnp.sum(wide_low.reshape(TOKENS, ADAPTER_COUNT, ADAPTER_RANK) * picker[:, :, None], axis=1).astype(jnp.bfloat16)
    dispersed_lowrank = (picker[:, :, None] * low_rank.astype(jnp.float32)[:, None, :]).reshape(TOKENS, ADAPTER_COUNT * ADAPTER_RANK).astype(jnp.bfloat16)
    frozen_output = jnp.dot(hidden, frozen_weight, preferred_element_type=jnp.float32)
    output = (frozen_output + adapter_scale * jnp.dot(dispersed_lowrank, flattened_output_maps, preferred_element_type=jnp.float32)).astype(jnp.bfloat16)
    frozen_gradient = jnp.dot(cotangent, frozen_weight.T, preferred_element_type=jnp.float32)
    wide_back = jnp.dot(cotangent, flattened_output_maps.T, preferred_element_type=jnp.float32)
    back_low = jnp.sum(wide_back.reshape(TOKENS, ADAPTER_COUNT, ADAPTER_RANK) * picker[:, :, None], axis=1).astype(jnp.bfloat16)
    dispersed_gradient = (picker[:, :, None] * back_low.astype(jnp.float32)[:, None, :]).reshape(TOKENS, ADAPTER_COUNT * ADAPTER_RANK).astype(jnp.bfloat16)
    adapter_rows = (adapter_scale * jnp.dot(dispersed_gradient, flattened_input_maps, preferred_element_type=jnp.float32)).astype(jnp.bfloat16)
    adapter_rows = lax.optimization_barrier(adapter_rows)
    hidden_gradient = (frozen_gradient + adapter_rows.astype(jnp.float32)).astype(jnp.bfloat16)
    input_map_gradient = adapter_scale * jnp.dot(dispersed_gradient.T, hidden, preferred_element_type=jnp.float32).reshape(ADAPTER_COUNT, ADAPTER_RANK, HIDDEN_UNITS)
    output_map_gradient = adapter_scale * jnp.dot(dispersed_lowrank.T, cotangent, preferred_element_type=jnp.float32).reshape(ADAPTER_COUNT, ADAPTER_RANK, MODEL_DIM)
    return output, hidden_gradient, input_map_gradient, output_map_gradient
```

```python
import functools

import jax
import jax.numpy as jnp
from jax import lax
from jax.experimental import pallas as pl
from jax.experimental.pallas import tpu as pltpu
from jax.sharding import PartitionSpec as P

adapter_scale = 0.5
vmem_bytes = 32 * 1024 * 1024
narrow_bits = (2, 8)


def partners(members, bit):
    return [(i, i ^ bit) for i in range(members)]


def swap(value, members, bit):
    return lax.ppermute(value, "tensor", partners(members, bit))


def forward_kernel(places, hidden_ref, weight_ref, *rest):
    out_ref = rest[-1]
    out_ref[0] = jnp.dot(hidden_ref[...], weight_ref[...], preferred_element_type=jnp.float32)


def forward_slabs(places, hidden, weight, width, earlier=()):
    tokens, depth = hidden.shape
    count = places.shape[0]
    return pl.pallas_call(
        forward_kernel,
        grid_spec=pltpu.PrefetchScalarGridSpec(
            num_scalar_prefetch=1,
            grid=(count,),
            in_specs=[
                pl.BlockSpec((tokens, depth), lambda j, places: (0, 0)),
                pl.BlockSpec((depth, width), lambda j, places: (0, places[j])),
            ]
            + [pl.BlockSpec(memory_space=pl.ANY)] * len(earlier),
            out_specs=pl.BlockSpec((1, tokens, width), lambda j, places: (j, 0, 0)),
        ),
        out_shape=jax.ShapeDtypeStruct((count, tokens, width), jnp.float32),
        compiler_params=pltpu.CompilerParams(vmem_limit_bytes=vmem_bytes),
        cost_estimate=pl.CostEstimate(
            flops=2 * count * tokens * depth * width,
            bytes_accessed=count * width * (2 * depth + 4 * tokens),
            transcendentals=0,
        ),
        name="forward_slabs",
    )(places, hidden, weight, *earlier)


def gradient_kernel(steps, places, slab_ref, first_ref, second_ref, start_ref, *rest):
    out_ref, total = rest[-2:]
    step = pl.program_id(0)
    across = (((1,), (1,)), ((), ()))
    term = lax.dot_general(
        slab_ref[0], first_ref[...], across, preferred_element_type=jnp.float32
    ) + lax.dot_general(slab_ref[1], second_ref[...], across, preferred_element_type=jnp.float32)

    @pl.when(step == 0)
    def _():
        total[...] = start_ref[...].astype(jnp.float32) + term

    @pl.when(step > 0)
    def _():
        total[...] += term

    @pl.when(step == steps - 1)
    def _():
        out_ref[...] = total[...].astype(out_ref.dtype)


def add_gradient(places, slabs, weight, start, dtype, earlier=()):
    count, tokens, width = slabs.shape
    depth = weight.shape[0]
    steps = count // 2
    return pl.pallas_call(
        functools.partial(gradient_kernel, steps),
        grid_spec=pltpu.PrefetchScalarGridSpec(
            num_scalar_prefetch=1,
            grid=(steps,),
            in_specs=[
                pl.BlockSpec((2, tokens, width), lambda j, places: (j, 0, 0)),
                pl.BlockSpec((depth, width), lambda j, places: (0, places[2 * j])),
                pl.BlockSpec((depth, width), lambda j, places: (0, places[2 * j + 1])),
                pl.BlockSpec((tokens, depth), lambda j, places: (0, 0)),
            ]
            + [pl.BlockSpec(memory_space=pl.ANY)] * len(earlier),
            out_specs=pl.BlockSpec((tokens, depth), lambda j, places: (0, 0)),
            scratch_shapes=[pltpu.VMEM((tokens, depth), jnp.float32)],
        ),
        out_shape=jax.ShapeDtypeStruct((tokens, depth), dtype),
        compiler_params=pltpu.CompilerParams(vmem_limit_bytes=vmem_bytes),
        cost_estimate=pl.CostEstimate(
            flops=2 * count * tokens * depth * width,
            bytes_accessed=2 * count * width * (depth + tokens),
            transcendentals=0,
        ),
        name="hidden_gradient",
    )(places, slabs, weight, weight, start, *earlier)


def whole_call(kernel, ins, out_shapes, earlier, name):
    return pl.pallas_call(
        kernel,
        in_specs=[pl.BlockSpec(memory_space=pltpu.VMEM)] * len(ins)
        + [pl.BlockSpec(memory_space=pl.ANY)] * len(earlier),
        out_specs=pl.BlockSpec(memory_space=pltpu.VMEM),
        out_shape=out_shapes,
        compiler_params=pltpu.CompilerParams(vmem_limit_bytes=vmem_bytes),
        name=name,
    )(*ins, *earlier)


def join_kernel(mine_ref, other_ref, *rest):
    rest[-1][...] = mine_ref[...] + other_ref[...].astype(jnp.float32)


def join(mine, other, earlier):
    shape = jax.ShapeDtypeStruct(mine.shape, jnp.float32)
    return whole_call(join_kernel, (mine, other), shape, earlier, "join")


def place_kernel(ff_slab, grads_ref, *rest):
    in_ref, out_ref = rest[-2:]
    grads = grads_ref[0].astype(jnp.float32)
    in_ref[...] = grads[:, :ff_slab].reshape(in_ref.shape)
    out_ref[...] = grads[:, ff_slab:].reshape(out_ref.shape)


def place_gradients(grads, resident, ff_slab, earlier):
    members, held_rows, width = grads.shape
    rank_width = held_rows // resident
    d_slab = width - ff_slab
    return pl.pallas_call(
        functools.partial(place_kernel, ff_slab),
        grid=(members,),
        in_specs=[pl.BlockSpec((1, held_rows, width), lambda m: (m, 0, 0))]
        + [pl.BlockSpec(memory_space=pl.ANY)] * len(earlier),
        out_specs=[
            pl.BlockSpec((resident, rank_width, ff_slab), lambda m: (0, 0, m)),
            pl.BlockSpec((resident, rank_width, d_slab), lambda m: (0, 0, m)),
        ],
        out_shape=[
            jax.ShapeDtypeStruct((resident, rank_width, members * ff_slab), jnp.float32),
            jax.ShapeDtypeStruct((resident, rank_width, members * d_slab), jnp.float32),
        ],
        compiler_params=pltpu.CompilerParams(vmem_limit_bytes=vmem_bytes),
        name="place_gradients",
    )(grads, *earlier)


def pair_kernel(ff_slab, maps_ref, hidden_ref, cotangent_ref, picker_ref, *rest):
    out_ref = rest[-1]
    adapters, _, tokens = picker_ref.shape
    rank_width = maps_ref.shape[0] // adapters
    across = (((1,), (1,)), ((), ()))
    low = lax.dot_general(
        maps_ref[:, :ff_slab], hidden_ref[...], across, preferred_element_type=jnp.float32
    )
    back = lax.dot_general(
        maps_ref[:, ff_slab:], cotangent_ref[...], across, preferred_element_type=jnp.float32
    )
    by_rank = (adapters, rank_width, tokens)
    out_ref[:rank_width] = jnp.sum(low.reshape(by_rank) * picker_ref[...], axis=0)
    out_ref[rank_width:] = jnp.sum(back.reshape(by_rank) * picker_ref[...], axis=0)


def low_rank_pair(maps, hidden, cotangent, picker, earlier):
    adapters, _, tokens = picker.shape
    rank_width = maps.shape[0] // adapters
    return pl.pallas_call(
        functools.partial(pair_kernel, hidden.shape[1]),
        in_specs=[pl.BlockSpec(memory_space=pltpu.VMEM)] * 4
        + [pl.BlockSpec(memory_space=pl.ANY)] * len(earlier),
        out_specs=pl.BlockSpec(memory_space=pltpu.VMEM),
        out_shape=jax.ShapeDtypeStruct((2 * rank_width, tokens), jnp.float32),
        compiler_params=pltpu.CompilerParams(vmem_limit_bytes=vmem_bytes),
        cost_estimate=pl.CostEstimate(
            flops=2 * maps.size * tokens,
            bytes_accessed=2 * (maps.size + hidden.size + cotangent.size),
            transcendentals=0,
        ),
        name="low_rank_pair",
    )(maps, hidden, cotangent, picker, *earlier)


def local(
    hidden,
    frozen_weight,
    adapter_input_maps,
    adapter_output_maps,
    adapter_per_block,
    rows_per_block,
    cotangent,
):
    members = lax.axis_size("tensor")
    me = lax.axis_index("tensor")
    tokens, ff_slab = hidden.shape
    d_slab = cotangent.shape[1]
    blocks = adapter_per_block.shape[0]
    block_len = tokens // blocks
    resident, rank_width, hidden_total = adapter_input_maps.shape
    adapters = resident * members
    held_rows = resident * rank_width
    bits = [1 << i for i in range(members.bit_length() - 1)]

    split_in = adapter_input_maps.reshape(held_rows, members, ff_slab).transpose(1, 0, 2)
    split_out = adapter_output_maps.reshape(held_rows, members, d_slab).transpose(1, 0, 2)
    packed = jnp.concatenate([split_in, split_out], axis=2)
    maps = lax.all_to_all(packed, "tensor", 0, 0, tiled=True).reshape(
        members * held_rows, ff_slab + d_slab
    )
    maps_in, maps_out = maps[:, :ff_slab], maps[:, ff_slab:]

    slabs = lax.all_gather(cotangent, "tensor", axis=0)

    def send(value, bit):
        wire = jnp.bfloat16 if bit in narrow_bits else jnp.float32
        return swap(value.astype(wire), members, bit)

    half = members // 2
    sums = {}
    groups = []
    earlier = (packed,)
    for first in (half, 0):
        offsets = list(range(first + half - 1, first - 1, -1))
        group = forward_slabs(
            jnp.bitwise_xor(me, jnp.array(offsets, jnp.int32)),
            hidden,
            frozen_weight,
            d_slab,
            earlier,
        )
        groups.append(group)
        part = {k: group[j] for j, k in enumerate(offsets)}
        for k in offsets[1::2]:
            sums[k] = part[k] + send(part[k ^ 1], 1)
        earlier = ()

    for bit in bits[1:-1]:
        for k in [k for k in sums if k % (2 * bit) == bit]:
            if k >= half or bit == bits[1]:
                sums[k ^ bit] = join(sums[k ^ bit], send(sums[k], bit), groups[1:])
    ready = (sums[half],) + tuple(
        sums[k] for k in sums if k < half and k % (2 * bits[1]) == 0
    )

    live = (jnp.arange(block_len)[None, :] < rows_per_block[:, None]).reshape(tokens)
    row_adapter = jnp.broadcast_to(adapter_per_block[:, None], (blocks, block_len)).reshape(tokens)
    picker = (
        (jnp.arange(adapters)[:, None] == row_adapter[None, :]) & live[None, :]
    ).astype(jnp.float32)[:, None, :]
    pair = low_rank_pair(maps, hidden, cotangent, picker, ready)
    for bit in bits:
        pair = pair + swap(pair, members, bit)
    pair = pair.astype(jnp.bfloat16).astype(jnp.float32)
    flat = (adapters * rank_width, tokens)
    low_spread = (picker * pair[None, :rank_width]).astype(jnp.bfloat16).reshape(flat)
    back_spread = (picker * pair[None, rank_width:]).astype(jnp.bfloat16).reshape(flat)

    grad_in = adapter_scale * jnp.dot(back_spread, hidden, preferred_element_type=jnp.float32)
    grad_out = adapter_scale * jnp.dot(low_spread, cotangent, preferred_element_type=jnp.float32)
    grads = jnp.concatenate(
        [grad_in.astype(jnp.bfloat16), grad_out.astype(jnp.bfloat16)], axis=1
    ).reshape(members, held_rows, ff_slab + d_slab)
    sent = (grads,)
    grads = lax.all_to_all(grads, "tensor", 0, 0, tiled=True)

    down = (((0,), (0,)), ((), ()))
    lora_rows = (
        adapter_scale
        * lax.dot_general(back_spread, maps_in, down, preferred_element_type=jnp.float32)
    ).astype(jnp.bfloat16)
    hidden_gradient = add_gradient(
        jnp.arange(members, dtype=jnp.int32), slabs, frozen_weight, lora_rows, jnp.bfloat16, sent
    )

    for bit in bits[2:-1]:
        for k in [k for k in sums if k < half and k % (2 * bit) == bit]:
            sums[k ^ bit] = join(sums[k ^ bit], send(sums[k], bit), (hidden_gradient,))
    output_sum = join(sums[0], send(sums[half], half), (hidden_gradient,))
    input_map_gradient, output_map_gradient = place_gradients(
        grads, resident, ff_slab, (hidden_gradient,)
    )
    adapter_output = adapter_scale * lax.dot_general(
        low_spread, maps_out, down, preferred_element_type=jnp.float32
    )
    output = (output_sum + adapter_output).astype(jnp.bfloat16)
    return (output, hidden_gradient, input_map_gradient, output_map_gradient)


def solution(mesh):
    in_specs = (
        P("parts", "tensor"),
        P("tensor", None),
        P(("parts", "tensor"), None, None),
        P(("parts", "tensor"), None, None),
        P("parts"),
        P("parts"),
        P("parts", "tensor"),
    )
    out_specs = (
        P("parts", "tensor"),
        P("parts", "tensor"),
        P(("parts", "tensor"), None, None),
        P(("parts", "tensor"), None, None),
    )
    return jax.shard_map(local, mesh=mesh, in_specs=in_specs, out_specs=out_specs, check_vma=False)
```

```python
import functools

import jax
import jax.numpy as jnp
from jax import lax
from jax.experimental import pallas as pl
from jax.experimental.pallas import tpu as pltpu
from jax.sharding import PartitionSpec as P

adapter_scale = 0.5
vmem_bytes = 32 * 1024 * 1024
narrow_bits = (2, 8)


def partners(members, bit):
    return [(i, i ^ bit) for i in range(members)]


def swap(value, members, bit):
    return lax.ppermute(value, "tensor", partners(members, bit))


def forward_kernel(places, hidden_ref, weight_ref, *rest):
    out_ref = rest[-1]
    out_ref[0] = jnp.dot(hidden_ref[...], weight_ref[...], preferred_element_type=jnp.float32)


def forward_slabs(places, hidden, weight, width, earlier=()):
    tokens, depth = hidden.shape
    count = places.shape[0]
    return pl.pallas_call(
        forward_kernel,
        grid_spec=pltpu.PrefetchScalarGridSpec(
            num_scalar_prefetch=1,
            grid=(count,),
            in_specs=[
                pl.BlockSpec((tokens, depth), lambda j, places: (0, 0)),
                pl.BlockSpec((depth, width), lambda j, places: (0, places[j])),
            ]
            + [pl.BlockSpec(memory_space=pl.ANY)] * len(earlier),
            out_specs=pl.BlockSpec((1, tokens, width), lambda j, places: (j, 0, 0)),
        ),
        out_shape=jax.ShapeDtypeStruct((count, tokens, width), jnp.float32),
        compiler_params=pltpu.CompilerParams(vmem_limit_bytes=vmem_bytes),
        cost_estimate=pl.CostEstimate(
            flops=2 * count * tokens * depth * width,
            bytes_accessed=count * width * (2 * depth + 4 * tokens),
            transcendentals=0,
        ),
        name="forward_slabs",
    )(places, hidden, weight, *earlier)


def gradient_kernel(steps, places, slab_ref, first_ref, second_ref, start_ref, *rest):
    out_ref, total = rest[-2:]
    step = pl.program_id(0)
    across = (((1,), (1,)), ((), ()))
    term = lax.dot_general(
        slab_ref[0], first_ref[...], across, preferred_element_type=jnp.float32
    ) + lax.dot_general(slab_ref[1], second_ref[...], across, preferred_element_type=jnp.float32)

    @pl.when(step == 0)
    def _():
        total[...] = start_ref[...].astype(jnp.float32) + term

    @pl.when(step > 0)
    def _():
        total[...] += term

    @pl.when(step == steps - 1)
    def _():
        out_ref[...] = total[...].astype(out_ref.dtype)


def add_gradient(places, slabs, weight, start, dtype, earlier=()):
    count, tokens, width = slabs.shape
    depth = weight.shape[0]
    steps = count // 2
    return pl.pallas_call(
        functools.partial(gradient_kernel, steps),
        grid_spec=pltpu.PrefetchScalarGridSpec(
            num_scalar_prefetch=1,
            grid=(steps,),
            in_specs=[
                pl.BlockSpec((2, tokens, width), lambda j, places: (j, 0, 0)),
                pl.BlockSpec((depth, width), lambda j, places: (0, places[2 * j])),
                pl.BlockSpec((depth, width), lambda j, places: (0, places[2 * j + 1])),
                pl.BlockSpec((tokens, depth), lambda j, places: (0, 0)),
            ]
            + [pl.BlockSpec(memory_space=pl.ANY)] * len(earlier),
            out_specs=pl.BlockSpec((tokens, depth), lambda j, places: (0, 0)),
            scratch_shapes=[pltpu.VMEM((tokens, depth), jnp.float32)],
        ),
        out_shape=jax.ShapeDtypeStruct((tokens, depth), dtype),
        compiler_params=pltpu.CompilerParams(vmem_limit_bytes=vmem_bytes),
        cost_estimate=pl.CostEstimate(
            flops=2 * count * tokens * depth * width,
            bytes_accessed=2 * count * width * (depth + tokens),
            transcendentals=0,
        ),
        name="hidden_gradient",
    )(places, slabs, weight, weight, start, *earlier)


def whole_call(kernel, ins, out_shapes, earlier, name):
    return pl.pallas_call(
        kernel,
        in_specs=[pl.BlockSpec(memory_space=pltpu.VMEM)] * len(ins)
        + [pl.BlockSpec(memory_space=pl.ANY)] * len(earlier),
        out_specs=pl.BlockSpec(memory_space=pltpu.VMEM),
        out_shape=out_shapes,
        compiler_params=pltpu.CompilerParams(vmem_limit_bytes=vmem_bytes),
        name=name,
    )(*ins, *earlier)


def join_kernel(mine_ref, other_ref, *rest):
    total = mine_ref[...] + other_ref[...].astype(jnp.float32)
    rest[-1][...] = total.astype(rest[-1].dtype)


def join(mine, other, earlier, dtype=jnp.float32):
    shape = jax.ShapeDtypeStruct(mine.shape, dtype)
    return whole_call(join_kernel, (mine, other), shape, earlier, "join")


def gate_kernel(value_ref, *rest):
    rest[-1][...] = value_ref[...]


def gate(value, earlier):
    shape = jax.ShapeDtypeStruct(value.shape, value.dtype)
    return whole_call(gate_kernel, (value,), shape, earlier, "gate")


def place_kernel(ff_slab, grads_ref, *rest):
    in_ref, out_ref = rest[-2:]
    resident, rank_width, _ = in_ref.shape
    count, _, width = grads_ref.shape
    d_slab = width - ff_slab
    for m in range(count):
        grads = grads_ref[m].astype(jnp.float32).reshape(resident, rank_width, width)
        in_ref[:, :, m * ff_slab : (m + 1) * ff_slab] = grads[:, :, :ff_slab]
        out_ref[:, :, m * d_slab : (m + 1) * d_slab] = grads[:, :, ff_slab:]


def place_gradients(grads, resident, ff_slab, earlier):
    members, held_rows, width = grads.shape
    rank_width = held_rows // resident
    d_slab = width - ff_slab
    return pl.pallas_call(
        functools.partial(place_kernel, ff_slab),
        grid=(members // 4,),
        in_specs=[pl.BlockSpec((4, held_rows, width), lambda m: (m, 0, 0))]
        + [pl.BlockSpec(memory_space=pl.ANY)] * len(earlier),
        out_specs=[
            pl.BlockSpec((resident, rank_width, 4 * ff_slab), lambda m: (0, 0, m)),
            pl.BlockSpec((resident, rank_width, 4 * d_slab), lambda m: (0, 0, m)),
        ],
        out_shape=[
            jax.ShapeDtypeStruct((resident, rank_width, members * ff_slab), jnp.float32),
            jax.ShapeDtypeStruct((resident, rank_width, members * d_slab), jnp.float32),
        ],
        compiler_params=pltpu.CompilerParams(vmem_limit_bytes=vmem_bytes),
        name="place_gradients",
    )(grads, *earlier)


def pair_kernel(ff_slab, maps_ref, hidden_ref, cotangent_ref, picker_ref, *rest):
    out_ref = rest[-1]
    adapters, _, tokens = picker_ref.shape
    rank_width = maps_ref.shape[0] // adapters
    across = (((1,), (1,)), ((), ()))
    low = lax.dot_general(
        maps_ref[:, :ff_slab], hidden_ref[...], across, preferred_element_type=jnp.float32
    )
    back = lax.dot_general(
        maps_ref[:, ff_slab:], cotangent_ref[...], across, preferred_element_type=jnp.float32
    )
    by_rank = (adapters, rank_width, tokens)
    out_ref[:rank_width] = jnp.sum(low.reshape(by_rank) * picker_ref[...], axis=0)
    out_ref[rank_width:] = jnp.sum(back.reshape(by_rank) * picker_ref[...], axis=0)


def low_rank_pair(maps, hidden, cotangent, picker, earlier):
    adapters, _, tokens = picker.shape
    rank_width = maps.shape[0] // adapters
    return pl.pallas_call(
        functools.partial(pair_kernel, hidden.shape[1]),
        in_specs=[pl.BlockSpec(memory_space=pltpu.VMEM)] * 4
        + [pl.BlockSpec(memory_space=pl.ANY)] * len(earlier),
        out_specs=pl.BlockSpec(memory_space=pltpu.VMEM),
        out_shape=jax.ShapeDtypeStruct((2 * rank_width, tokens), jnp.float32),
        compiler_params=pltpu.CompilerParams(vmem_limit_bytes=vmem_bytes),
        cost_estimate=pl.CostEstimate(
            flops=2 * maps.size * tokens,
            bytes_accessed=2 * (maps.size + hidden.size + cotangent.size),
            transcendentals=0,
        ),
        name="low_rank_pair",
    )(maps, hidden, cotangent, picker, *earlier)


def local(
    hidden,
    frozen_weight,
    adapter_input_maps,
    adapter_output_maps,
    adapter_per_block,
    rows_per_block,
    cotangent,
):
    members = lax.axis_size("tensor")
    me = lax.axis_index("tensor")
    tokens, ff_slab = hidden.shape
    d_slab = cotangent.shape[1]
    blocks = adapter_per_block.shape[0]
    block_len = tokens // blocks
    resident, rank_width, hidden_total = adapter_input_maps.shape
    adapters = resident * members
    held_rows = resident * rank_width
    bits = [1 << i for i in range(members.bit_length() - 1)]

    split_in = adapter_input_maps.reshape(held_rows, members, ff_slab).transpose(1, 0, 2)
    split_out = adapter_output_maps.reshape(held_rows, members, d_slab).transpose(1, 0, 2)
    packed = jnp.concatenate([split_in, split_out], axis=2)
    maps = lax.all_to_all(packed, "tensor", 0, 0, tiled=True).reshape(
        members * held_rows, ff_slab + d_slab
    )
    maps_in, maps_out = maps[:, :ff_slab], maps[:, ff_slab:]

    slabs = lax.all_gather(cotangent, "tensor", axis=0)

    def send(value, bit):
        wire = jnp.bfloat16 if bit in narrow_bits else jnp.float32
        return swap(value.astype(wire), members, bit)

    half = members // 2
    sums = {}
    groups = []
    earlier = (packed,)
    for first in (half, 0):
        offsets = list(range(first + half - 1, first - 1, -1))
        group = forward_slabs(
            jnp.bitwise_xor(me, jnp.array(offsets, jnp.int32)),
            hidden,
            frozen_weight,
            d_slab,
            earlier,
        )
        groups.append(group)
        part = {k: group[j] for j, k in enumerate(offsets)}
        for k in offsets[1::2]:
            sums[k] = part[k] + send(part[k ^ 1], 1)
        earlier = ()

    for bit in bits[1:-1]:
        for k in [k for k in sums if k % (2 * bit) == bit]:
            if k >= half or bit == bits[1]:
                last = k ^ bit == half and bit == bits[-2]
                dtype = jnp.bfloat16 if last and half in narrow_bits else jnp.float32
                sums[k ^ bit] = join(sums[k ^ bit], send(sums[k], bit), groups[1:], dtype)
    last_sent = send(sums[half], half)
    ready = (sums[half],) + tuple(
        sums[k] for k in sums if k < half and k % (2 * bits[1]) == 0
    )

    live = (jnp.arange(block_len)[None, :] < rows_per_block[:, None]).reshape(tokens)
    row_adapter = jnp.broadcast_to(adapter_per_block[:, None], (blocks, block_len)).reshape(tokens)
    picker = (
        (jnp.arange(adapters)[:, None] == row_adapter[None, :]) & live[None, :]
    ).astype(jnp.float32)[:, None, :]
    pair = low_rank_pair(maps, hidden, cotangent, picker, ready)
    for bit in bits:
        pair = pair + swap(pair, members, bit)
    pair = gate(pair, (last_sent,))
    pair = pair.astype(jnp.bfloat16).astype(jnp.float32)
    flat = (adapters * rank_width, tokens)
    low_spread = (picker * pair[None, :rank_width]).astype(jnp.bfloat16).reshape(flat)
    back_spread = (picker * pair[None, rank_width:]).astype(jnp.bfloat16).reshape(flat)

    grad_in = adapter_scale * jnp.dot(back_spread, hidden, preferred_element_type=jnp.float32)
    grad_out = adapter_scale * jnp.dot(low_spread, cotangent, preferred_element_type=jnp.float32)
    grads = jnp.concatenate(
        [grad_in.astype(jnp.bfloat16), grad_out.astype(jnp.bfloat16)], axis=1
    ).reshape(members, held_rows, ff_slab + d_slab)
    sent = (grads,)
    grads = lax.all_to_all(grads, "tensor", 0, 0, tiled=True)

    down = (((0,), (0,)), ((), ()))
    lora_rows = (
        adapter_scale
        * lax.dot_general(back_spread, maps_in, down, preferred_element_type=jnp.float32)
    ).astype(jnp.bfloat16)
    hidden_gradient = add_gradient(
        jnp.arange(members, dtype=jnp.int32), slabs, frozen_weight, lora_rows, jnp.bfloat16, sent
    )

    for bit in bits[2:-1]:
        for k in [k for k in sums if k < half and k % (2 * bit) == bit]:
            sums[k ^ bit] = join(sums[k ^ bit], send(sums[k], bit), (hidden_gradient,))
    output_sum = join(sums[0], last_sent, (hidden_gradient,))
    input_map_gradient, output_map_gradient = place_gradients(
        grads, resident, ff_slab, (hidden_gradient,)
    )
    adapter_output = adapter_scale * lax.dot_general(
        low_spread, maps_out, down, preferred_element_type=jnp.float32
    )
    output = (output_sum + adapter_output).astype(jnp.bfloat16)
    return (output, hidden_gradient, input_map_gradient, output_map_gradient)


def solution(mesh):
    in_specs = (
        P("parts", "tensor"),
        P("tensor", None),
        P(("parts", "tensor"), None, None),
        P(("parts", "tensor"), None, None),
        P("parts"),
        P("parts"),
        P("parts", "tensor"),
    )
    out_specs = (
        P("parts", "tensor"),
        P("parts", "tensor"),
        P(("parts", "tensor"), None, None),
        P(("parts", "tensor"), None, None),
    )
    return jax.shard_map(local, mesh=mesh, in_specs=in_specs, out_specs=out_specs, check_vma=False)
```
